256 devices in a mesh: lat: 64 (over z, x_hi, y), lon: 4 (over x_lo, core).
Axes of the slice: x: 4 (x_hi: 2, x_lo: 2; x = x_hi * 2 + x_lo), y: 4, z: 8, core: 2. Of those that a mesh axis runs over, the one named last changes fastest.
Arguments:
- field: bfloat16 [256, 1920, 256], P('lat', 'lon'), may hold values from -6 to 6
- filter_blocks: bfloat16 [256, 9, 5, 128], P('lat'), may hold values from -0.3125 to 0.3125
- filter_scales: float32 [256, 9], P('lat'), may hold values from 0.3 to 3
- lon_offsets: int32 [256], P('lat'), may hold values from -64 to 63, as said below
- lon_widths: int32 [256], P('lat'), may hold values from 1 to 128
- halo_rows: int32 [256], P('lat'), may hold values from 1 to 2
- mixing: bfloat16 [2304, 256], replicated, may hold values from -0.125 to 0.125
Outputs:
- mixed: bfloat16 [256, 1920, 256], P('lat', 'lon')
The draws below stay inside these ranges and needn't reach their ends.
Inputs may be any that keep to these rules, and one draw needn't show every extreme that they name: lon_offsets[i] >= -64 and lon_offsets[i] + lon_widths[i] <= 64.
All inputs are finite; a program needn't handle non-finite values.
Results may differ from the reference program's by a relative error of at most 0.0049.
Values may be sent and summed in bfloat16 or wider, within the bound.
A program may use at most 192 MiB of HBM per device.

```python
import math
import jax
import jax.numpy as jnp
from jax import lax

CH = 256
OUTC = 256
BASIS = 9
HROWS = 2
REACH = 64
BLOCK = 120
TAPS = 5
W_MAX = 128
NLAT = 256
NLON = 1920


def shared_widths(key):
    widths = jax.random.randint(key, (NLAT,), 1, 2 * REACH + 1).astype(jnp.int32)
    widths = widths.at[0].set(2 * REACH)
    widths = widths.at[1].set(1)
    return widths


def draw_lon_widths(key, part):
    widths = shared_widths(key)
    return widths


def draw_lon_offsets(key, part):
    widths = shared_widths(key)
    key = jax.random.fold_in(key, 5)
    spread = jax.random.randint(key, (NLAT,), 0, 2 * REACH + 1 - widths).astype(jnp.int32)
    spread = spread.at[0].set(0)
    spread = spread.at[1].set(2 * REACH - 1)
    return (spread - REACH).astype(jnp.int32)


def draw_halo_rows(key, part):
    key = jax.random.fold_in(key, 7)
    rows = jax.random.randint(key, (NLAT,), 1, HROWS + 1).astype(jnp.int32)
    rows = rows.at[0].set(HROWS)
    rows = rows.at[1].set(1)
    return rows


def block_scale(own_key, dims, pieces, smallest, top_value):
    level = 1.0
    for position, parts in pieces:
        heights = jax.random.uniform(jax.random.fold_in(jax.random.fold_in(own_key, 6), position), (parts,), jnp.float32, smallest / len(pieces), top_value / len(pieces))
        level = level * jnp.repeat(jnp.exp(heights), dims[position] // parts).reshape((-1,) + (1,) * (len(dims) - 1 - position))
    return level


def noise(stream_key, shape, deviation, limit, cuts=(), held_as=jnp.bfloat16):
    level = block_scale(stream_key, shape, cuts, -0.22, 0.18) if cuts else 1.0
    array = jax.random.normal(stream_key, shape, jnp.float32) * deviation * level
    return jnp.minimum(jnp.maximum(array, -limit), limit).astype(held_as)


def setup_inputs(seed: int = 0) -> dict:
    arg_keys = jax.random.split(jax.random.key(seed), 8)
    return {
        "field": noise(arg_keys[0], (NLAT, NLON, CH), 1.0, 6.0, ((0, 64), (1, 4))),
        "filter_blocks": noise(arg_keys[1], (NLAT, BASIS, TAPS, W_MAX), (TAPS * REACH) ** -0.5, 0.3125, ((0, 64),)),
        "filter_scales": jnp.clip(jnp.exp(math.log(3.0) - 2.3025851 * jax.random.uniform(arg_keys[2], (NLAT, BASIS), jnp.float32) ** block_scale(arg_keys[2], (NLAT, BASIS), ((0, 64),), -0.2, 0.2)), 0.3, 3.0),
        "lon_offsets": draw_lon_offsets(jax.random.fold_in(arg_keys[7], 71), 0),
        "lon_widths": draw_lon_widths(jax.random.fold_in(arg_keys[7], 71), 0),
        "halo_rows": draw_halo_rows(jax.random.fold_in(arg_keys[7], 71), 0),
        "mixing": noise(arg_keys[6], (BASIS * CH, OUTC), (BASIS * CH) ** -0.5, 0.125),
    }


def make_band(block, offset, width, hrow):
    cols = jnp.arange(BLOCK, dtype=jnp.int32)[:, None]
    inputs = jnp.arange(BLOCK + 2 * REACH, dtype=jnp.int32)[None, :]
    entry = inputs - cols - REACH - offset
    valid = (entry >= 0) & (entry < width)
    clipped = jnp.clip(entry, 0, 2 * REACH - 1)
    picked = block[:, :, clipped]
    taps = jnp.abs(jnp.arange(2 * HROWS + 1, dtype=jnp.int32) - HROWS) <= hrow
    keep = valid[None, None, :, :] & taps[None, :, None, None]
    return jnp.where(keep, picked, jnp.zeros_like(picked))


def reference(field, filter_blocks, filter_scales, lon_offsets, lon_widths, halo_rows, mixing):
    wrapped = jnp.concatenate([field[:, NLON - REACH:], field, field[:, :REACH]], 1)
    padded = jnp.pad(wrapped, ((HROWS, HROWS), (0, 0), (0, 0)))
    weights = mixing.astype(jnp.float32).reshape(BASIS, CH, OUTC)
    nblocks = NLON // BLOCK

    def one_row(inputs):
        row_index, block, scale, offset, width, hrow = inputs
        rows = lax.dynamic_slice_in_dim(padded, row_index, 2 * HROWS + 1, 0)
        band = make_band(block, offset, width, hrow).astype(jnp.float32)
        windows = jnp.stack([rows[:, part * BLOCK:part * BLOCK + BLOCK + 2 * REACH] for part in range(nblocks)], 1).astype(jnp.float32)
        summed = jnp.einsum('ktjq,tbqc->bkjc', band, windows)
        conv = (summed * scale[None, :, None, None]).astype(jnp.bfloat16)
        result = jnp.einsum('bkjc,kco->bjo', conv.astype(jnp.float32), weights)
        return result.astype(jnp.bfloat16).reshape(NLON, OUTC)

    indices = jnp.arange(NLAT, dtype=jnp.int32)
    return lax.map(one_row, (indices, filter_blocks, filter_scales, lon_offsets, lon_widths, halo_rows))
```

```python
import functools

import jax
import jax.numpy as jnp
from jax import lax
from jax.experimental import pallas as pl
from jax.experimental.pallas import tpu as pltpu
from jax.sharding import PartitionSpec as P

MESH = pl.DeviceIdType.MESH
BASIS = 9
TAPS = 5
HROWS = 2
REACH = 64
SPAN = 2 * REACH
BLOCK = 32
GROUP = 5
F32 = jnp.float32
BF16 = jnp.bfloat16

OWN_TAPS = ((2, 3, 4), (1, 2, 3, 4), (0, 1, 2, 3), (0, 1, 2))
AWAY_TAPS = ((0, 1), (0,), (4,), (3, 4))


def kernel(
    n_lat, n_lon,
    x_ref, f_ref, s_ref, off_ref, wid_ref, halo_ref, w_hbm, out,
    ext, lines, moved, a_own, a_away, acc, conv, tail, w_ref,
    own_sem, near_s, near_r, far_s, far_r, lon_s, lon_r, rel_s, rel_r,
):
    rows, cols, chans = x_ref.shape
    la, lo = lax.axis_index("lat"), lax.axis_index("lon")
    west, east = lax.rem(lo + n_lon - 1, n_lon), lax.rem(lo + 1, n_lon)
    has_n, has_s = la > 0, la < n_lat - 1
    far_cuts = ((0, 64), (cols - 64, 64), (64, 160), (224, 160), (384, 32))

    barrier = pltpu.get_barrier_semaphore()
    for lon in (west, east):
        pl.semaphore_signal(barrier, inc=1, device_id=(la, lon), device_id_type=MESH)

    @pl.when(has_n)
    def _():
        pl.semaphore_signal(barrier, inc=1, device_id=(la - 1, lo), device_id_type=MESH)

    @pl.when(has_s)
    def _():
        pl.semaphore_signal(barrier, inc=1, device_id=(la + 1, lo), device_id_type=MESH)

    own = pltpu.make_async_copy(
        x_ref, ext.at[pl.ds(HROWS, rows), pl.ds(REACH, cols)], own_sem.at[0]
    )
    own.start()
    weights = pltpu.make_async_copy(w_hbm, w_ref, own_sem.at[1])
    weights.start()

    peers = 2 + jnp.where(has_n, 1, 0) + jnp.where(has_s, 1, 0)
    pl.semaphore_wait(barrier, peers)

    def near_copy(d):
        src, dst, to = ((rows - 1, 1, la + 1), (0, rows + HROWS, la - 1))[d]
        return pltpu.make_async_remote_copy(
            x_ref.at[src], ext.at[dst, pl.ds(REACH, cols)],
            near_s.at[d], near_r.at[d], device_id=(to, lo), device_id_type=MESH,
        )

    def far_copy(d, p):
        src, dst, to = ((rows - 2, 0, la + 1), (1, rows + HROWS + 1, la - 1))[d]
        at, size = far_cuts[p]
        return pltpu.make_async_remote_copy(
            x_ref.at[src, pl.ds(at, size)], ext.at[dst, pl.ds(REACH + at, size)],
            far_s.at[d, p], far_r.at[d, p], device_id=(to, lo), device_id_type=MESH,
        )

    def lon_copy(d):
        at, to, land = ((cols - REACH, east, 0), (0, west, cols + REACH))[d]
        return pltpu.make_async_remote_copy(
            x_ref.at[:, pl.ds(at, REACH)], ext.at[pl.ds(HROWS, rows), pl.ds(land, REACH)],
            lon_s.at[d], lon_r.at[d], device_id=(la, to), device_id_type=MESH,
        )

    def relay(r, d):
        row = (1, rows + HROWS, 0, rows + HROWS + 1)[r]
        at, to, land = ((cols, east, 0), (REACH, west, cols + REACH))[d]
        return pltpu.make_async_remote_copy(
            ext.at[row, pl.ds(at, REACH)], ext.at[row, pl.ds(land, REACH)],
            rel_s.at[r, d], rel_r.at[r, d], device_id=(la, to), device_id_type=MESH,
        )

    sends = (has_s, has_n)
    comes = (has_n, has_s)
    pieces = range(len(far_cuts))

    for d in range(2):
        @pl.when(sends[d])
        def _():
            near_copy(d).start()

    for d in range(2):
        lon_copy(d).start()

    for d in range(2):
        @pl.when(sends[d])
        def _():
            for p in pieces:
                far_copy(d, p).start()

    @pl.when(jnp.logical_not(has_n))
    def _():
        ext[0:HROWS] = jnp.zeros((HROWS, cols + SPAN, chans), BF16)

    @pl.when(jnp.logical_not(has_s))
    def _():
        ext[rows + HROWS:] = jnp.zeros((HROWS, cols + SPAN, chans), BF16)

    tall = BASIS * BLOCK
    lane = lax.broadcasted_iota(jnp.int32, (BLOCK, SPAN), 1)
    step = lax.broadcasted_iota(jnp.int32, (BLOCK, SPAN), 0)
    entry = lax.broadcasted_iota(jnp.int32, (SPAN, SPAN), 0)
    place = lax.broadcasted_iota(jnp.int32, (SPAN, SPAN), 1)
    n_lines = lines.shape[0]
    line_at = lax.broadcasted_iota(jnp.int32, (n_lines, SPAN), 0)
    line_tap = (line_at - line_at // (TAPS * rows) * (TAPS * rows)) // rows

    lines[n_lines - 8:] = jnp.zeros((8, SPAN), F32)
    for k in range(BASIS):
        for t in range(TAPS):
            at = (k * TAPS + t) * rows
            lines[at:at + rows] = f_ref[k, t].astype(F32)
    for i in range(rows):
        hit = (place == entry + off_ref[i] + REACH) & (entry < wid_ref[i])
        mover = jnp.where(hit, 1.0, 0.0).astype(BF16)
        shifted = jnp.dot(lines[...].astype(BF16), mover, preferred_element_type=F32)
        moved[i] = jnp.where(jnp.abs(line_tap - HROWS) <= halo_ref[i], shifted, 0.0)

    def unit(ref, i, j, k, taps):
        at = k * BLOCK
        rest = jnp.zeros((BLOCK, SPAN), F32)
        for u, t in enumerate(taps):
            row = (k * TAPS + t) * rows + i
            line = jnp.broadcast_to(moved[i, row:row + 1], (BLOCK, SPAN))
            skew = pltpu.roll(line, 0, 1, stride=1, stride_axis=0)
            head = jnp.where(lane >= step, skew, 0.0)
            ref[j, at:at + BLOCK, u * SPAN:(u + 1) * SPAN] = head.astype(BF16)
            spot = lane - u * BLOCK
            turned = pltpu.roll(skew, u * BLOCK, 1) if u else skew
            rest = jnp.where((spot >= 0) & (spot < step), turned, rest)
        n = len(taps)
        ref[j, at:at + BLOCK, n * SPAN:(n + 1) * SPAN] = rest.astype(BF16)

    def window(rows_in, b):
        at = b * BLOCK
        heads = [ext[r, at:at + SPAN] for r in rows_in]
        rests = [ext[r, at + SPAN:at + SPAN + BLOCK] for r in rows_in]
        return jnp.concatenate(heads + rests, 0)

    def part(ref, i, taps, b):
        depth = len(taps) * (SPAN + BLOCK)
        return jnp.dot(
            ref[i, :, 0:depth], window([i + t for t in taps], b), preferred_element_type=F32
        )

    def own_part(i, b):
        acc[i, b] = part(a_own, i, OWN_TAPS[i], b)

    def finish(i, b, ref, slot, at):
        total = acc[i, b] + part(a_away, i, AWAY_TAPS[i], b)
        for k in range(BASIS):
            scaled = total[k * BLOCK:(k + 1) * BLOCK] * s_ref[i, k]
            ref[slot, at:at + BLOCK, k * chans:(k + 1) * chans] = scaled.astype(BF16)

    blocks = cols // BLOCK
    for i in range(rows):
        for k in range(BASIS):
            unit(a_own, i, i, k, OWN_TAPS[i])
            unit(a_away, i, i, k, AWAY_TAPS[i])
    own.wait()
    for d in range(2):
        lon_copy(d).wait_recv()
    for b in range(blocks):
        own_part(1, b)
        own_part(2, b)

    def pass_on(d, r, waits):
        @pl.when(comes[d])
        def _():
            waits()
            for e in range(2):
                relay(r, e).start()

    def wait_relay(d, r):
        @pl.when(comes[d])
        def _():
            for e in range(2):
                relay(r, e).wait_recv()

    for d in range(2):
        pass_on(d, d, lambda: near_copy(d).wait_recv())
    for b in range(blocks):
        own_part(0, b)
        own_part(3, b)
    weights.wait()
    for d in range(2):
        wait_relay(d, d)
    for b in range(blocks):
        finish(1, b, conv, 0, b * BLOCK)
        finish(2, b, conv, 1, b * BLOCK)

    def edges(d):
        far_copy(d, 0).wait_recv()
        far_copy(d, 1).wait_recv()

    for d in range(2):
        pass_on(d, 2 + d, lambda: edges(d))
    for i in (1, 2):
        out[i] = jnp.dot(conv[i - 1], w_ref[...], preferred_element_type=F32).astype(BF16)

    for d in range(2):
        wait_relay(d, 2 + d)
    size = GROUP * BLOCK
    half = 4 * chans
    for g in range(blocks // GROUP):
        for d in range(2):
            @pl.when(comes[d])
            def _():
                far_copy(d, 2 + g).wait_recv()
        for u in range(GROUP):
            finish(0, g * GROUP + u, tail, 0, u * BLOCK)
            finish(3, g * GROUP + u, tail, 1, u * BLOCK)
        both = tail[...].reshape(2 * size, BASIS * chans)
        result = jnp.dot(both[:, :half], w_ref[:half], preferred_element_type=F32)
        result += jnp.dot(both[:, half:], w_ref[half:], preferred_element_type=F32)
        out[0, g * size:(g + 1) * size] = result[:size].astype(BF16)
        out[3, g * size:(g + 1) * size] = result[size:].astype(BF16)

    for d in range(2):
        @pl.when(sends[d])
        def _():
            near_copy(d).wait_send()
            for p in pieces:
                far_copy(d, p).wait_send()
    for d in range(2):
        lon_copy(d).wait_send()
    for d in range(2):
        @pl.when(comes[d])
        def _():
            for r in (d, 2 + d):
                for e in range(2):
                    relay(r, e).wait_send()


def hand_over(src, dst, sem):
    copy = pltpu.make_async_copy(src, dst, sem)
    copy.start()
    copy.wait()


def solution(mesh):
    n_lat, n_lon = mesh.shape["lat"], mesh.shape["lon"]

    def on_device(field, filter_blocks, filter_scales, lon_offsets, lon_widths, halo_rows, mixing):
        rows, cols, chans = field.shape
        outs = mixing.shape[1]
        wide = cols + SPAN
        blocks = cols // BLOCK
        tall = BASIS * BLOCK
        n_lines = -(-BASIS * TAPS * rows // 8) * 8
        smem = pl.BlockSpec(memory_space=pltpu.SMEM)
        hbm = pl.BlockSpec(memory_space=pl.ANY)
        dma = pltpu.SemaphoreType.DMA
        filters = jnp.transpose(filter_blocks, (1, 2, 0, 3))
        mixed = pl.pallas_call(
            functools.partial(kernel, n_lat, n_lon),
            out_shape=pltpu.VMEM((rows, cols, outs), BF16),
            in_specs=[hbm, pl.BlockSpec(memory_space=pltpu.VMEM), smem, smem, smem, smem, hbm],
            out_specs=pl.BlockSpec(memory_space=pltpu.VMEM),
            scratch_shapes=[
                pltpu.VMEM((rows + 2 * HROWS, wide, chans), BF16),
                pltpu.VMEM((n_lines, SPAN), F32),
                pltpu.VMEM((rows, n_lines, SPAN), F32),
                pltpu.VMEM((rows, tall, 5 * SPAN), BF16),
                pltpu.VMEM((rows, tall, 3 * SPAN), BF16),
                pltpu.VMEM((rows, blocks, tall, chans), F32),
                pltpu.VMEM((2, cols, BASIS * chans), BF16),
                pltpu.VMEM((2, GROUP * BLOCK, BASIS * chans), BF16),
                pltpu.VMEM((BASIS * chans, outs), BF16),
                dma((2,)),
                dma((2,)), dma((2,)),
                dma((2, 5)), dma((2, 5)),
                dma((2,)), dma((2,)),
                dma((4, 2)), dma((4, 2)),
            ],
            compiler_params=pltpu.CompilerParams(
                collective_id=0, has_side_effects=True, vmem_limit_bytes=56 * 2**20
            ),
            cost_estimate=pl.CostEstimate(
                flops=13_000_000_000, bytes_accessed=4_000_000, transcendentals=0
            ),
            name="disco",
        )(field, filters, filter_scales, lon_offsets, lon_widths, halo_rows, mixing)

        return pl.pallas_call(
            hand_over,
            out_shape=jax.ShapeDtypeStruct(mixed.shape, mixed.dtype),
            in_specs=[pl.BlockSpec(memory_space=pltpu.VMEM)],
            out_specs=hbm,
            scratch_shapes=[dma],
            name="hand_over",
        )(mixed)

    return jax.shard_map(
        on_device,
        mesh=mesh,
        in_specs=(
            P("lat", "lon", None),
            P("lat", None, None, None),
            P("lat", None),
            P("lat"),
            P("lat"),
            P("lat"),
            P(),
        ),
        out_specs=P("lat", "lon", None),
        check_vma=False,
    )
```

```python
import functools

import jax
import jax.numpy as jnp
from jax import lax
from jax.experimental import pallas as pl
from jax.experimental.pallas import tpu as pltpu
from jax.sharding import PartitionSpec as P

MESH = pl.DeviceIdType.MESH
BASIS = 9
TAPS = 5
HROWS = 2
REACH = 64
SPAN = 2 * REACH
BLOCK = 32
GROUP = 5
F32 = jnp.float32
BF16 = jnp.bfloat16

OWN_TAPS = ((2, 3, 4), (1, 2, 3, 4), (0, 1, 2, 3), (0, 1, 2))
AWAY_TAPS = ((0, 1), (0,), (4,), (3, 4))
FAR_CUTS = ((64, 160), (224, 160), (384, 32))


def kernel(
    n_lat, n_lon,
    x_ref, f_ref, s_ref, off_ref, wid_ref, halo_ref, w_hbm, out,
    ext, lines, moved, a_own, a_away, acc, conv, tail, w_ref,
    own_sem, edge_s, edge_r, near_s, near_r, far_s, far_r, lon_s, lon_r, rel_s, rel_r,
):
    rows, cols, chans = x_ref.shape
    la, lo = lax.axis_index("lat"), lax.axis_index("lon")
    west, east = lax.rem(lo + n_lon - 1, n_lon), lax.rem(lo + 1, n_lon)
    has_n, has_s = la > 0, la < n_lat - 1
    far_cuts = FAR_CUTS

    barrier = pltpu.get_barrier_semaphore()
    for lon in (west, east):
        pl.semaphore_signal(barrier, inc=1, device_id=(la, lon), device_id_type=MESH)

    @pl.when(has_n)
    def _():
        pl.semaphore_signal(barrier, inc=1, device_id=(la - 1, lo), device_id_type=MESH)

    @pl.when(has_s)
    def _():
        pl.semaphore_signal(barrier, inc=1, device_id=(la + 1, lo), device_id_type=MESH)

    own = pltpu.make_async_copy(
        x_ref, ext.at[pl.ds(HROWS, rows), pl.ds(REACH, cols)], own_sem.at[0]
    )
    own.start()
    weights = pltpu.make_async_copy(w_hbm, w_ref, own_sem.at[1])
    weights.start()

    tall = BASIS * BLOCK
    lane = lax.broadcasted_iota(jnp.int32, (BLOCK, SPAN), 1)
    step = lax.broadcasted_iota(jnp.int32, (BLOCK, SPAN), 0)
    entry = lax.broadcasted_iota(jnp.int32, (SPAN, SPAN), 0)
    place = lax.broadcasted_iota(jnp.int32, (SPAN, SPAN), 1)
    n_lines = lines.shape[0]
    line_at = lax.broadcasted_iota(jnp.int32, (n_lines, SPAN), 0)
    line_tap = (line_at - line_at // (TAPS * rows) * (TAPS * rows)) // rows

    lines[n_lines - 8:] = jnp.zeros((8, SPAN), F32)
    for k in range(BASIS):
        for t in range(TAPS):
            at = (k * TAPS + t) * rows
            lines[at:at + rows] = f_ref[k, t].astype(F32)
    for i in range(rows):
        hit = (place == entry + off_ref[i] + REACH) & (entry < wid_ref[i])
        mover = jnp.where(hit, 1.0, 0.0).astype(BF16)
        shifted = jnp.dot(lines[...].astype(BF16), mover, preferred_element_type=F32)
        moved[i] = jnp.where(jnp.abs(line_tap - HROWS) <= halo_ref[i], shifted, 0.0)

    def unit(ref, i, j, k, taps):
        at = k * BLOCK
        rest = jnp.zeros((BLOCK, SPAN), F32)
        for u, t in enumerate(taps):
            row = (k * TAPS + t) * rows + i
            line = jnp.broadcast_to(moved[i, row:row + 1], (BLOCK, SPAN))
            skew = pltpu.roll(line, 0, 1, stride=1, stride_axis=0)
            head = jnp.where(lane >= step, skew, 0.0)
            ref[j, at:at + BLOCK, u * SPAN:(u + 1) * SPAN] = head.astype(BF16)
            spot = lane - u * BLOCK
            turned = pltpu.roll(skew, u * BLOCK, 1) if u else skew
            rest = jnp.where((spot >= 0) & (spot < step), turned, rest)
        n = len(taps)
        ref[j, at:at + BLOCK, n * SPAN:(n + 1) * SPAN] = rest.astype(BF16)

    for i in range(rows):
        for k in range(BASIS):
            unit(a_own, i, i, k, OWN_TAPS[i])
            unit(a_away, i, i, k, AWAY_TAPS[i])

    peers = 2 + jnp.where(has_n, 1, 0) + jnp.where(has_s, 1, 0)
    pl.semaphore_wait(barrier, peers)

    def lat_copy(d, near, far, at, size, send, recv):
        src, dst, to = ((rows - 2, 0, la + 1), (0, rows + HROWS, la - 1))[d]
        skip, count = (0, 2) if near and far else ((1 - d, 1) if near else (d, 1))
        return pltpu.make_async_remote_copy(
            x_ref.at[pl.ds(src + skip, count), pl.ds(at, size)],
            ext.at[pl.ds(dst + skip, count), pl.ds(REACH + at, size)],
            send, recv, device_id=(to, lo), device_id_type=MESH,
        )

    def edge_copy(d, e):
        at = (0, cols - REACH)[e]
        return lat_copy(d, True, True, at, REACH, edge_s.at[d, e], edge_r.at[d, e])

    def near_copy(d):
        return lat_copy(d, True, False, REACH, cols - SPAN, near_s.at[d], near_r.at[d])

    def far_copy(d, p):
        at, size = far_cuts[p]
        return lat_copy(d, False, True, at, size, far_s.at[d, p], far_r.at[d, p])

    def lon_copy(d):
        at, to, land = ((cols - REACH, east, 0), (0, west, cols + REACH))[d]
        return pltpu.make_async_remote_copy(
            x_ref.at[:, pl.ds(at, REACH)], ext.at[pl.ds(HROWS, rows), pl.ds(land, REACH)],
            lon_s.at[d], lon_r.at[d], device_id=(la, to), device_id_type=MESH,
        )

    def relay(d, e):
        row = (0, rows + HROWS)[d]
        at, to, land = ((cols, east, 0), (REACH, west, cols + REACH))[e]
        return pltpu.make_async_remote_copy(
            ext.at[pl.ds(row, HROWS), pl.ds(at, REACH)],
            ext.at[pl.ds(row, HROWS), pl.ds(land, REACH)],
            rel_s.at[d, e], rel_r.at[d, e], device_id=(la, to), device_id_type=MESH,
        )

    sends = (has_s, has_n)
    comes = (has_n, has_s)
    pieces = range(len(far_cuts))

    def guarded(conds, action):
        for d in range(2):
            @pl.when(conds[d])
            def _():
                action(d)

    def send_edges(d):
        for e in range(2):
            edge_copy(d, e).start()

    def send_rest(d):
        near_copy(d).start()
        for p in pieces:
            far_copy(d, p).start()

    guarded(sends, send_edges)
    for d in range(2):
        lon_copy(d).start()
    guarded(sends, send_rest)

    @pl.when(jnp.logical_not(has_n))
    def _():
        ext[0:HROWS] = jnp.zeros((HROWS, cols + SPAN, chans), BF16)

    @pl.when(jnp.logical_not(has_s))
    def _():
        ext[rows + HROWS:] = jnp.zeros((HROWS, cols + SPAN, chans), BF16)

    def window(rows_in, b):
        at = b * BLOCK
        heads = [ext[r, at:at + SPAN] for r in rows_in]
        rests = [ext[r, at + SPAN:at + SPAN + BLOCK] for r in rows_in]
        return jnp.concatenate(heads + rests, 0)

    def part(ref, i, taps, b):
        depth = len(taps) * (SPAN + BLOCK)
        return jnp.dot(
            ref[i, :, 0:depth], window([i + t for t in taps], b), preferred_element_type=F32
        )

    def own_part(i, b):
        acc[i, b] = part(a_own, i, OWN_TAPS[i], b)

    def finish(i, b, ref, slot, at):
        total = acc[i, b] + part(a_away, i, AWAY_TAPS[i], b)
        for k in range(BASIS):
            scaled = total[k * BLOCK:(k + 1) * BLOCK] * s_ref[i, k]
            ref[slot, at:at + BLOCK, k * chans:(k + 1) * chans] = scaled.astype(BF16)

    blocks = cols // BLOCK
    inner = range(REACH // BLOCK, blocks - REACH // BLOCK)
    outer = [b for b in range(blocks) if b not in inner]
    own.wait()
    for b in inner:
        own_part(0, b)
        own_part(3, b)

    def pass_edges(d):
        for e in range(2):
            edge_copy(d, e).wait_recv()
        for e in range(2):
            relay(d, e).start()

    guarded(comes, pass_edges)

    for b in inner:
        own_part(1, b)
        own_part(2, b)
    for d in range(2):
        lon_copy(d).wait_recv()
    for b in outer:
        for i in range(rows):
            own_part(i, b)
    weights.wait()

    def take_corners(d):
        for e in range(2):
            relay(d, e).wait_recv()

    guarded(comes, lambda d: near_copy(d).wait_recv())
    for b in inner:
        finish(1, b, conv, 0, b * BLOCK)
        finish(2, b, conv, 1, b * BLOCK)
    guarded(comes, take_corners)
    for b in outer:
        finish(1, b, conv, 0, b * BLOCK)
        finish(2, b, conv, 1, b * BLOCK)

    def mix(ref, i, slot, at, size):
        mixed = jnp.dot(ref[slot, 0:size], w_ref[...], preferred_element_type=F32)
        out[i, at:at + size] = mixed.astype(BF16)

    size = GROUP * BLOCK
    for g in range(blocks // GROUP):
        guarded(comes, lambda d: far_copy(d, g).wait_recv())
        for u in range(GROUP):
            finish(0, g * GROUP + u, tail, 0, u * BLOCK)
            finish(3, g * GROUP + u, tail, 1, u * BLOCK)
        if g == 0:
            mix(conv, 1, 0, 0, cols)
            mix(conv, 2, 1, 0, cols)
        for slot, i in ((0, 0), (1, 3)):
            mix(tail, i, slot, g * size, size)

    def drain(d):
        for e in range(2):
            edge_copy(d, e).wait_send()
        near_copy(d).wait_send()
        for p in pieces:
            far_copy(d, p).wait_send()

    guarded(sends, drain)
    for d in range(2):
        lon_copy(d).wait_send()

    def drain_relays(d):
        for e in range(2):
            relay(d, e).wait_send()

    guarded(comes, drain_relays)


def solution(mesh):
    n_lat, n_lon = mesh.shape["lat"], mesh.shape["lon"]

    def on_device(field, filter_blocks, filter_scales, lon_offsets, lon_widths, halo_rows, mixing):
        rows, cols, chans = field.shape
        outs = mixing.shape[1]
        wide = cols + SPAN
        blocks = cols // BLOCK
        tall = BASIS * BLOCK
        n_lines = -(-BASIS * TAPS * rows // 8) * 8
        smem = pl.BlockSpec(memory_space=pltpu.SMEM)
        hbm = pl.BlockSpec(memory_space=pl.ANY)
        dma = pltpu.SemaphoreType.DMA
        filters = jnp.transpose(filter_blocks, (1, 2, 0, 3))
        return pl.pallas_call(
            functools.partial(kernel, n_lat, n_lon),
            out_shape=pltpu.VMEM((rows, cols, outs), BF16),
            in_specs=[hbm, pl.BlockSpec(memory_space=pltpu.VMEM), smem, smem, smem, smem, hbm],
            out_specs=pl.BlockSpec(memory_space=pltpu.VMEM),
            scratch_shapes=[
                pltpu.VMEM((rows + 2 * HROWS, wide, chans), BF16),
                pltpu.VMEM((n_lines, SPAN), F32),
                pltpu.VMEM((rows, n_lines, SPAN), F32),
                pltpu.VMEM((rows, tall, 5 * SPAN), BF16),
                pltpu.VMEM((rows, tall, 3 * SPAN), BF16),
                pltpu.VMEM((rows, blocks, tall, chans), F32),
                pltpu.VMEM((2, cols, BASIS * chans), BF16),
                pltpu.VMEM((2, GROUP * BLOCK, BASIS * chans), BF16),
                pltpu.VMEM((BASIS * chans, outs), BF16),
                dma((2,)),
                dma((2, 2)), dma((2, 2)),
                dma((2,)), dma((2,)),
                dma((2, len(FAR_CUTS))), dma((2, len(FAR_CUTS))),
                dma((2,)), dma((2,)),
                dma((2, 2)), dma((2, 2)),
            ],
            compiler_params=pltpu.CompilerParams(
                collective_id=0, has_side_effects=True, vmem_limit_bytes=56 * 2**20
            ),
            cost_estimate=pl.CostEstimate(
                flops=13_000_000_000, bytes_accessed=4_000_000, transcendentals=0
            ),
            name="disco",
        )(field, filters, filter_scales, lon_offsets, lon_widths, halo_rows, mixing)

    return jax.shard_map(
        on_device,
        mesh=mesh,
        in_specs=(
            P("lat", "lon", None),
            P("lat", None, None, None),
            P("lat", None),
            P("lat"),
            P("lat"),
            P("lat"),
            P(),
        ),
        out_specs=P("lat", "lon", None),
        check_vma=False,
    )
```

```python
import functools

import jax
import jax.numpy as jnp
from jax import lax
from jax.experimental import pallas as pl
from jax.experimental.pallas import tpu as pltpu
from jax.sharding import PartitionSpec as P

MESH = pl.DeviceIdType.MESH
BASIS = 9
TAPS = 5
HROWS = 2
REACH = 64
SPAN = 2 * REACH
BLOCK = 32
F32 = jnp.float32
BF16 = jnp.bfloat16

OWN_TAPS = ((2, 3, 4), (1, 2, 3, 4), (0, 1, 2, 3), (0, 1, 2))
AWAY_TAPS = ((0, 1), (0,), (4,), (3, 4))
FAR_CUTS = ((64, 160), (224, 160), (384, 32))
STAGES = ((2, 5), (5, 10), (10, 15))


def kernel(
    n_lat, n_lon,
    x_ref, f_ref, s_ref, off_ref, wid_ref, halo_ref, w_hbm, out,
    ext, lines, moved, a_own, a_away, acc, conv, tail, edge, w_ref,
    own_sem, edge_s, edge_r, near_s, near_r, far_s, far_r, lon_s, lon_r, rel_s, rel_r,
):
    rows, cols, chans = x_ref.shape
    la, lo = lax.axis_index("lat"), lax.axis_index("lon")
    west, east = lax.rem(lo + n_lon - 1, n_lon), lax.rem(lo + 1, n_lon)
    has_n, has_s = la > 0, la < n_lat - 1
    far_cuts = FAR_CUTS

    barrier = pltpu.get_barrier_semaphore()
    for lon in (west, east):
        pl.semaphore_signal(barrier, inc=1, device_id=(la, lon), device_id_type=MESH)

    @pl.when(has_n)
    def _():
        pl.semaphore_signal(barrier, inc=1, device_id=(la - 1, lo), device_id_type=MESH)

    @pl.when(has_s)
    def _():
        pl.semaphore_signal(barrier, inc=1, device_id=(la + 1, lo), device_id_type=MESH)

    own = pltpu.make_async_copy(
        x_ref, ext.at[pl.ds(HROWS, rows), pl.ds(REACH, cols)], own_sem.at[0]
    )
    own.start()
    weights = pltpu.make_async_copy(w_hbm, w_ref, own_sem.at[1])
    weights.start()

    tall = BASIS * BLOCK
    lane = lax.broadcasted_iota(jnp.int32, (BLOCK, SPAN), 1)
    step = lax.broadcasted_iota(jnp.int32, (BLOCK, SPAN), 0)
    entry = lax.broadcasted_iota(jnp.int32, (SPAN, SPAN), 0)
    place = lax.broadcasted_iota(jnp.int32, (SPAN, SPAN), 1)
    n_lines = lines.shape[0]
    line_at = lax.broadcasted_iota(jnp.int32, (n_lines, SPAN), 0)
    line_tap = (line_at - line_at // (TAPS * rows) * (TAPS * rows)) // rows

    lines[n_lines - 8:] = jnp.zeros((8, SPAN), F32)
    for k in range(BASIS):
        for t in range(TAPS):
            at = (k * TAPS + t) * rows
            lines[at:at + rows] = f_ref[k, t].astype(F32)
    for i in range(rows):
        hit = (place == entry + off_ref[i] + REACH) & (entry < wid_ref[i])
        mover = jnp.where(hit, 1.0, 0.0).astype(BF16)
        shifted = jnp.dot(lines[...].astype(BF16), mover, preferred_element_type=F32)
        moved[i] = jnp.where(jnp.abs(line_tap - HROWS) <= halo_ref[i], shifted, 0.0)

    def unit(ref, i, j, k, taps):
        at = k * BLOCK
        rest = jnp.zeros((BLOCK, SPAN), F32)
        for u, t in enumerate(taps):
            row = (k * TAPS + t) * rows + i
            line = jnp.broadcast_to(moved[i, row:row + 1], (BLOCK, SPAN))
            skew = pltpu.roll(line, 0, 1, stride=1, stride_axis=0)
            head = jnp.where(lane >= step, skew, 0.0)
            ref[j, at:at + BLOCK, u * SPAN:(u + 1) * SPAN] = head.astype(BF16)
            spot = lane - u * BLOCK
            turned = pltpu.roll(skew, u * BLOCK, 1) if u else skew
            rest = jnp.where((spot >= 0) & (spot < step), turned, rest)
        n = len(taps)
        ref[j, at:at + BLOCK, n * SPAN:(n + 1) * SPAN] = rest.astype(BF16)

    for i in range(rows):
        for k in range(BASIS):
            unit(a_own, i, i, k, OWN_TAPS[i])
            unit(a_away, i, i, k, AWAY_TAPS[i])

    peers = 2 + jnp.where(has_n, 1, 0) + jnp.where(has_s, 1, 0)
    pl.semaphore_wait(barrier, peers)

    def lat_copy(d, near, far, at, size, send, recv):
        src, dst, to = ((rows - 2, 0, la + 1), (0, rows + HROWS, la - 1))[d]
        skip, count = (0, 2) if near and far else ((1 - d, 1) if near else (d, 1))
        return pltpu.make_async_remote_copy(
            x_ref.at[pl.ds(src + skip, count), pl.ds(at, size)],
            ext.at[pl.ds(dst + skip, count), pl.ds(REACH + at, size)],
            send, recv, device_id=(to, lo), device_id_type=MESH,
        )

    def edge_copy(d, e):
        at = (0, cols - REACH)[e]
        return lat_copy(d, True, True, at, REACH, edge_s.at[d, e], edge_r.at[d, e])

    def near_copy(d):
        return lat_copy(d, True, False, REACH, cols - SPAN, near_s.at[d], near_r.at[d])

    def far_copy(d, p):
        at, size = far_cuts[p]
        return lat_copy(d, False, True, at, size, far_s.at[d, p], far_r.at[d, p])

    def lon_copy(d):
        at, to, land = ((cols - REACH, east, 0), (0, west, cols + REACH))[d]
        return pltpu.make_async_remote_copy(
            x_ref.at[:, pl.ds(at, REACH)], ext.at[pl.ds(HROWS, rows), pl.ds(land, REACH)],
            lon_s.at[d], lon_r.at[d], device_id=(la, to), device_id_type=MESH,
        )

    def relay(d, e):
        row = (0, rows + HROWS)[d]
        at, to, land = ((cols, east, 0), (REACH, west, cols + REACH))[e]
        return pltpu.make_async_remote_copy(
            ext.at[pl.ds(row, HROWS), pl.ds(at, REACH)],
            ext.at[pl.ds(row, HROWS), pl.ds(land, REACH)],
            rel_s.at[d, e], rel_r.at[d, e], device_id=(la, to), device_id_type=MESH,
        )

    sends = (has_s, has_n)
    comes = (has_n, has_s)
    pieces = range(len(far_cuts))

    def guarded(conds, action):
        for d in range(2):
            @pl.when(conds[d])
            def _():
                action(d)

    for d in range(2):
        lon_copy(d).start()
    for e in range(2):
        guarded(sends, lambda d: edge_copy(d, e).start())
    guarded(sends, lambda d: near_copy(d).start())
    for p in pieces:
        guarded(sends, lambda d: far_copy(d, p).start())

    @pl.when(jnp.logical_not(has_n))
    def _():
        ext[0:HROWS] = jnp.zeros((HROWS, cols + SPAN, chans), BF16)

    @pl.when(jnp.logical_not(has_s))
    def _():
        ext[rows + HROWS:] = jnp.zeros((HROWS, cols + SPAN, chans), BF16)

    def window(rows_in, b):
        at = b * BLOCK
        heads = [ext[r, at:at + SPAN] for r in rows_in]
        rests = [ext[r, at + SPAN:at + SPAN + BLOCK] for r in rows_in]
        return jnp.concatenate(heads + rests, 0)

    def part(ref, i, taps, b):
        depth = len(taps) * (SPAN + BLOCK)
        return jnp.dot(
            ref[i, :, 0:depth], window([i + t for t in taps], b), preferred_element_type=F32
        )

    def own_part(i, b):
        acc[i, b] = part(a_own, i, OWN_TAPS[i], b)

    def finish(i, b, ref, at):
        total = acc[i, b] + part(a_away, i, AWAY_TAPS[i], b)
        for k in range(BASIS):
            scaled = total[k * BLOCK:(k + 1) * BLOCK] * s_ref[i, k]
            ref[at:at + BLOCK, k * chans:(k + 1) * chans] = scaled.astype(BF16)

    blocks = cols // BLOCK
    inner = range(REACH // BLOCK, blocks - REACH // BLOCK)
    outer = [b for b in range(blocks) if b not in inner]
    own.wait()
    for b in inner:
        own_part(0, b)
        own_part(3, b)
    for b in inner:
        own_part(1, b)
        own_part(2, b)

    def pass_edges(d):
        for e in range(2):
            edge_copy(d, e).wait_recv()
        for e in range(2):
            relay(d, e).start()

    guarded(comes, pass_edges)
    weights.wait()
    guarded(comes, lambda d: near_copy(d).wait_recv())
    n_in = len(inner) * BLOCK
    for n, b in enumerate(inner):
        finish(1, b, conv, n * BLOCK)
        finish(2, b, conv, n_in + n * BLOCK)

    def mix(ref, at, size, lands):
        mixed = jnp.dot(ref[at:at + size], w_ref[...], preferred_element_type=F32).astype(BF16)
        at = 0
        for i, b, count in lands:
            out[i, b * BLOCK:(b + count) * BLOCK] = mixed[at:at + count * BLOCK]
            at += count * BLOCK

    def take_corners(d):
        for e in range(2):
            relay(d, e).wait_recv()

    for g, (lo_b, hi_b) in enumerate(STAGES[:-1]):
        guarded(comes, lambda d: far_copy(d, g).wait_recv())
        count = hi_b - lo_b
        for b in range(lo_b, hi_b):
            finish(0, b, tail, (b - lo_b) * BLOCK)
            finish(3, b, tail, (count + b - lo_b) * BLOCK)
        if g == 0:
            mix(conv, 0, n_in, [(1, inner[0], len(inner))])
            mix(conv, n_in, n_in, [(2, inner[0], len(inner))])
        for n, i in enumerate((0, 3)):
            mix(tail, n * count * BLOCK, count * BLOCK, [(i, lo_b, count)])

    for d in range(2):
        lon_copy(d).wait_recv()
    for b in outer:
        for i in range(rows):
            own_part(i, b)

    guarded(comes, take_corners)
    for n, b in enumerate(outer):
        finish(1, b, edge, n * BLOCK)
        finish(2, b, edge, (len(outer) + n) * BLOCK)
    guarded(comes, lambda d: far_copy(d, len(STAGES) - 1).wait_recv())
    lo_b, hi_b = STAGES[-1]
    ends = list(range(lo_b, hi_b)) + list(range(inner[0]))
    base = 2 * len(outer)
    for n, b in enumerate(ends):
        finish(0, b, edge, (base + n) * BLOCK)
        finish(3, b, edge, (base + len(ends) + n) * BLOCK)
    for n, i in enumerate((1, 2)):
        side = inner[0]
        mix(edge, n * len(outer) * BLOCK, len(outer) * BLOCK,
            [(i, 0, side), (i, blocks - side, side)])
    for n, i in enumerate((0, 3)):
        mix(edge, (base + n * len(ends)) * BLOCK, len(ends) * BLOCK,
            [(i, lo_b, hi_b - lo_b), (i, 0, inner[0])])

    def drain(d):
        for e in range(2):
            edge_copy(d, e).wait_send()
        near_copy(d).wait_send()
        for p in pieces:
            far_copy(d, p).wait_send()

    guarded(sends, drain)
    for d in range(2):
        lon_copy(d).wait_send()

    def drain_relays(d):
        for e in range(2):
            relay(d, e).wait_send()

    guarded(comes, drain_relays)


def solution(mesh):
    n_lat, n_lon = mesh.shape["lat"], mesh.shape["lon"]

    def on_device(field, filter_blocks, filter_scales, lon_offsets, lon_widths, halo_rows, mixing):
        rows, cols, chans = field.shape
        outs = mixing.shape[1]
        wide = cols + SPAN
        blocks = cols // BLOCK
        tall = BASIS * BLOCK
        n_lines = -(-BASIS * TAPS * rows // 8) * 8
        smem = pl.BlockSpec(memory_space=pltpu.SMEM)
        hbm = pl.BlockSpec(memory_space=pl.ANY)
        dma = pltpu.SemaphoreType.DMA
        filters = jnp.transpose(filter_blocks, (1, 2, 0, 3))
        return pl.pallas_call(
            functools.partial(kernel, n_lat, n_lon),
            out_shape=pltpu.VMEM((rows, cols, outs), BF16),
            in_specs=[hbm, pl.BlockSpec(memory_space=pltpu.VMEM), smem, smem, smem, smem, hbm],
            out_specs=pl.BlockSpec(memory_space=pltpu.VMEM),
            scratch_shapes=[
                pltpu.VMEM((rows + 2 * HROWS, wide, chans), BF16),
                pltpu.VMEM((n_lines, SPAN), F32),
                pltpu.VMEM((rows, n_lines, SPAN), F32),
                pltpu.VMEM((rows, tall, 5 * SPAN), BF16),
                pltpu.VMEM((rows, tall, 3 * SPAN), BF16),
                pltpu.VMEM((rows, blocks, tall, chans), F32),
                pltpu.VMEM((2 * (cols - SPAN), BASIS * chans), BF16),
                pltpu.VMEM((2 * 5 * BLOCK, BASIS * chans), BF16),
                pltpu.VMEM((22 * BLOCK, BASIS * chans), BF16),
                pltpu.VMEM((BASIS * chans, outs), BF16),
                dma((2,)),
                dma((2, 2)), dma((2, 2)),
                dma((2,)), dma((2,)),
                dma((2, len(FAR_CUTS))), dma((2, len(FAR_CUTS))),
                dma((2,)), dma((2,)),
                dma((2, 2)), dma((2, 2)),
            ],
            compiler_params=pltpu.CompilerParams(
                collective_id=0, has_side_effects=True, vmem_limit_bytes=56 * 2**20
            ),
            cost_estimate=pl.CostEstimate(
                flops=13_000_000_000, bytes_accessed=4_000_000, transcendentals=0
            ),
            name="disco",
        )(field, filters, filter_scales, lon_offsets, lon_widths, halo_rows, mixing)

    return jax.shard_map(
        on_device,
        mesh=mesh,
        in_specs=(
            P("lat", "lon", None),
            P("lat", None, None, None),
            P("lat", None),
            P("lat"),
            P("lat"),
            P("lat"),
            P(),
        ),
        out_specs=P("lat", "lon", None),
        check_vma=False,
    )
```

```python
import functools

import jax
import jax.numpy as jnp
from jax import lax
from jax.experimental import pallas as pl
from jax.experimental.pallas import tpu as pltpu
from jax.sharding import PartitionSpec as P

MESH = pl.DeviceIdType.MESH
BASIS = 9
TAPS = 5
HROWS = 2
REACH = 64
SPAN = 2 * REACH
BLOCK = 32
F32 = jnp.float32
BF16 = jnp.bfloat16

OWN_TAPS = ((2, 3, 4), (1, 2, 3, 4), (0, 1, 2, 3), (0, 1, 2))
AWAY_TAPS = ((0, 1), (0,), (4,), (3, 4))
FAR_CUTS = ((64, 160), (224, 160), (384, 32))
STAGES = ((2, 5), (5, 10), (10, 15))


def kernel(
    n_lat, n_lon,
    x_ref, f_ref, s_ref, off_ref, wid_ref, halo_ref, w_hbm, out,
    ext, lines, moved, a_own, a_away, acc, conv, tail, edge, w_ref,
    own_sem, edge_s, edge_r, near_s, near_r, far_s, far_r, lon_s, lon_r, rel_s, rel_r,
):
    rows, cols, chans = x_ref.shape
    la, lo = lax.axis_index("lat"), lax.axis_index("lon")
    west, east = lax.rem(lo + n_lon - 1, n_lon), lax.rem(lo + 1, n_lon)
    has_n, has_s = la > 0, la < n_lat - 1
    far_cuts = FAR_CUTS

    barrier = pltpu.get_barrier_semaphore()
    for lon in (west, east):
        pl.semaphore_signal(barrier, inc=1, device_id=(la, lon), device_id_type=MESH)

    @pl.when(has_n)
    def _():
        pl.semaphore_signal(barrier, inc=1, device_id=(la - 1, lo), device_id_type=MESH)

    @pl.when(has_s)
    def _():
        pl.semaphore_signal(barrier, inc=1, device_id=(la + 1, lo), device_id_type=MESH)

    own = pltpu.make_async_copy(
        x_ref, ext.at[pl.ds(HROWS, rows), pl.ds(REACH, cols)], own_sem.at[0]
    )
    own.start()
    weights = pltpu.make_async_copy(w_hbm, w_ref, own_sem.at[1])
    weights.start()

    tall = BASIS * BLOCK
    lane = lax.broadcasted_iota(jnp.int32, (BLOCK, SPAN), 1)
    step = lax.broadcasted_iota(jnp.int32, (BLOCK, SPAN), 0)
    entry = lax.broadcasted_iota(jnp.int32, (SPAN, SPAN), 0)
    place = lax.broadcasted_iota(jnp.int32, (SPAN, SPAN), 1)
    n_lines = lines.shape[0]
    line_at = lax.broadcasted_iota(jnp.int32, (n_lines, SPAN), 0)
    line_tap = (line_at - line_at // (TAPS * rows) * (TAPS * rows)) // rows

    lines[n_lines - 8:] = jnp.zeros((8, SPAN), F32)
    for k in range(BASIS):
        for t in range(TAPS):
            at = (k * TAPS + t) * rows
            lines[at:at + rows] = f_ref[k, t].astype(F32)
    for i in range(rows):
        hit = (place == entry + off_ref[i] + REACH) & (entry < wid_ref[i])
        mover = jnp.where(hit, 1.0, 0.0).astype(BF16)
        shifted = jnp.dot(lines[...].astype(BF16), mover, preferred_element_type=F32)
        moved[i] = jnp.where(jnp.abs(line_tap - HROWS) <= halo_ref[i], shifted, 0.0)

    def unit(ref, i, j, k, taps):
        at = k * BLOCK
        rest = jnp.zeros((BLOCK, SPAN), F32)
        for u, t in enumerate(taps):
            row = (k * TAPS + t) * rows + i
            line = jnp.broadcast_to(moved[i, row:row + 1], (BLOCK, SPAN))
            skew = pltpu.roll(line, 0, 1, stride=1, stride_axis=0)
            head = jnp.where(lane >= step, skew, 0.0)
            ref[j, at:at + BLOCK, u * SPAN:(u + 1) * SPAN] = head.astype(BF16)
            spot = lane - u * BLOCK
            turned = pltpu.roll(skew, u * BLOCK, 1) if u else skew
            rest = jnp.where((spot >= 0) & (spot < step), turned, rest)
        n = len(taps)
        ref[j, at:at + BLOCK, n * SPAN:(n + 1) * SPAN] = rest.astype(BF16)

    for i in range(rows):
        for k in range(BASIS):
            unit(a_own, i, i, k, OWN_TAPS[i])
            unit(a_away, i, i, k, AWAY_TAPS[i])

    peers = 2 + jnp.where(has_n, 1, 0) + jnp.where(has_s, 1, 0)
    pl.semaphore_wait(barrier, peers)

    def lat_copy(d, near, far, at, size, send, recv):
        src, dst, to = ((rows - 2, 0, la + 1), (0, rows + HROWS, la - 1))[d]
        skip, count = (0, 2) if near and far else ((1 - d, 1) if near else (d, 1))
        return pltpu.make_async_remote_copy(
            x_ref.at[pl.ds(src + skip, count), pl.ds(at, size)],
            ext.at[pl.ds(dst + skip, count), pl.ds(REACH + at, size)],
            send, recv, device_id=(to, lo), device_id_type=MESH,
        )

    def edge_copy(d, e):
        at = (0, cols - REACH)[e]
        return lat_copy(d, True, True, at, REACH, edge_s.at[d, e], edge_r.at[d, e])

    def near_copy(d):
        return lat_copy(d, True, False, REACH, cols - SPAN, near_s.at[d], near_r.at[d])

    def far_copy(d, p):
        at, size = far_cuts[p]
        return lat_copy(d, False, True, at, size, far_s.at[d, p], far_r.at[d, p])

    def lon_copy(d):
        at, to, land = ((cols - REACH, east, 0), (0, west, cols + REACH))[d]
        return pltpu.make_async_remote_copy(
            x_ref.at[:, pl.ds(at, REACH)], ext.at[pl.ds(HROWS, rows), pl.ds(land, REACH)],
            lon_s.at[d], lon_r.at[d], device_id=(la, to), device_id_type=MESH,
        )

    def relay(d, e):
        row = (0, rows + HROWS)[d]
        at, to, land = ((cols, east, 0), (REACH, west, cols + REACH))[e]
        return pltpu.make_async_remote_copy(
            ext.at[pl.ds(row, HROWS), pl.ds(at, REACH)],
            ext.at[pl.ds(row, HROWS), pl.ds(land, REACH)],
            rel_s.at[d, e], rel_r.at[d, e], device_id=(la, to), device_id_type=MESH,
        )

    sends = (has_s, has_n)
    comes = (has_n, has_s)
    pieces = range(len(far_cuts))

    def guarded(conds, action):
        for d in range(2):
            @pl.when(conds[d])
            def _():
                action(d)

    for d in range(2):
        lon_copy(d).start()
    for e in range(2):
        guarded(sends, lambda d: edge_copy(d, e).start())
    guarded(sends, lambda d: near_copy(d).start())
    for p in pieces:
        guarded(sends, lambda d: far_copy(d, p).start())

    @pl.when(jnp.logical_not(has_n))
    def _():
        ext[0:HROWS] = jnp.zeros((HROWS, cols + SPAN, chans), BF16)

    @pl.when(jnp.logical_not(has_s))
    def _():
        ext[rows + HROWS:] = jnp.zeros((HROWS, cols + SPAN, chans), BF16)

    def window(rows_in, b):
        at = b * BLOCK
        heads = [ext[r, at:at + SPAN] for r in rows_in]
        rests = [ext[r, at + SPAN:at + SPAN + BLOCK] for r in rows_in]
        return jnp.concatenate(heads + rests, 0)

    def part(ref, i, taps, b):
        depth = len(taps) * (SPAN + BLOCK)
        return jnp.dot(
            ref[i, :, 0:depth], window([i + t for t in taps], b), preferred_element_type=F32
        )

    def own_part(i, b):
        acc[i, b] = part(a_own, i, OWN_TAPS[i], b)

    def finish(i, b, ref, at):
        total = acc[i, b] + part(a_away, i, AWAY_TAPS[i], b)
        for k in range(BASIS):
            scaled = total[k * BLOCK:(k + 1) * BLOCK] * s_ref[i, k]
            ref[at:at + BLOCK, k * chans:(k + 1) * chans] = scaled.astype(BF16)

    blocks = cols // BLOCK
    inner = range(REACH // BLOCK, blocks - REACH // BLOCK)
    outer = [b for b in range(blocks) if b not in inner]
    own.wait()
    for b in inner:
        own_part(0, b)
        own_part(3, b)
    for b in inner:
        own_part(1, b)
        own_part(2, b)

    def pass_edges(d):
        for e in range(2):
            edge_copy(d, e).wait_recv()
        for e in range(2):
            relay(d, e).start()

    guarded(comes, pass_edges)
    weights.wait()
    guarded(comes, lambda d: near_copy(d).wait_recv())
    n_in = len(inner) * BLOCK
    for n, b in enumerate(inner):
        finish(1, b, conv, n * BLOCK)
        finish(2, b, conv, n_in + n * BLOCK)

    def mix(ref, at, size, lands):
        mixed = jnp.dot(ref[at:at + size], w_ref[...], preferred_element_type=F32).astype(BF16)
        at = 0
        for i, b, count in lands:
            out[i, b * BLOCK:(b + count) * BLOCK] = mixed[at:at + count * BLOCK]
            at += count * BLOCK

    def take_corners(d):
        for e in range(2):
            relay(d, e).wait_recv()

    for g, (lo_b, hi_b) in enumerate(STAGES[:-1]):
        guarded(comes, lambda d: far_copy(d, g).wait_recv())
        count = hi_b - lo_b
        for b in range(lo_b, hi_b):
            finish(0, b, tail, (b - lo_b) * BLOCK)
            finish(3, b, tail, (count + b - lo_b) * BLOCK)
        if g == 0:
            mix(conv, 0, n_in, [(1, inner[0], len(inner))])
            mix(conv, n_in, n_in, [(2, inner[0], len(inner))])
        for n, i in enumerate((0, 3)):
            mix(tail, n * count * BLOCK, count * BLOCK, [(i, lo_b, count)])

    for d in range(2):
        lon_copy(d).wait_recv()
    for b in outer:
        for i in range(rows):
            own_part(i, b)

    guarded(comes, take_corners)
    side = inner[0]
    lo_b, hi_b = STAGES[-1]
    ends = list(range(lo_b, hi_b)) + list(range(side))
    base = len(outer)
    half = (base + len(ends)) * BLOCK
    for n, b in enumerate(outer):
        finish(1, b, edge, n * BLOCK)
        finish(2, b, edge, half + n * BLOCK)
    guarded(comes, lambda d: far_copy(d, len(STAGES) - 1).wait_recv())
    for n, b in enumerate(ends):
        finish(0, b, edge, (base + n) * BLOCK)
        finish(3, b, edge, half + (base + n) * BLOCK)
    for at, i, j in ((0, 1, 0), (half, 2, 3)):
        mix(edge, at, half,
            [(i, 0, side), (i, blocks - side, side), (j, lo_b, hi_b - lo_b), (j, 0, side)])

    def drain(d):
        for e in range(2):
            edge_copy(d, e).wait_send()
        near_copy(d).wait_send()
        for p in pieces:
            far_copy(d, p).wait_send()

    guarded(sends, drain)
    for d in range(2):
        lon_copy(d).wait_send()

    def drain_relays(d):
        for e in range(2):
            relay(d, e).wait_send()

    guarded(comes, drain_relays)


def solution(mesh):
    n_lat, n_lon = mesh.shape["lat"], mesh.shape["lon"]

    def on_device(field, filter_blocks, filter_scales, lon_offsets, lon_widths, halo_rows, mixing):
        rows, cols, chans = field.shape
        outs = mixing.shape[1]
        wide = cols + SPAN
        blocks = cols // BLOCK
        tall = BASIS * BLOCK
        n_lines = -(-BASIS * TAPS * rows // 8) * 8
        smem = pl.BlockSpec(memory_space=pltpu.SMEM)
        hbm = pl.BlockSpec(memory_space=pl.ANY)
        dma = pltpu.SemaphoreType.DMA
        filters = jnp.transpose(filter_blocks, (1, 2, 0, 3))
        return pl.pallas_call(
            functools.partial(kernel, n_lat, n_lon),
            out_shape=pltpu.VMEM((rows, cols, outs), BF16),
            in_specs=[hbm, pl.BlockSpec(memory_space=pltpu.VMEM), smem, smem, smem, smem, hbm],
            out_specs=pl.BlockSpec(memory_space=pltpu.VMEM),
            scratch_shapes=[
                pltpu.VMEM((rows + 2 * HROWS, wide, chans), BF16),
                pltpu.VMEM((n_lines, SPAN), F32),
                pltpu.VMEM((rows, n_lines, SPAN), F32),
                pltpu.VMEM((rows, tall, 5 * SPAN), BF16),
                pltpu.VMEM((rows, tall, 3 * SPAN), BF16),
                pltpu.VMEM((rows, blocks, tall, chans), F32),
                pltpu.VMEM((2 * (cols - SPAN), BASIS * chans), BF16),
                pltpu.VMEM((2 * 5 * BLOCK, BASIS * chans), BF16),
                pltpu.VMEM((22 * BLOCK, BASIS * chans), BF16),
                pltpu.VMEM((BASIS * chans, outs), BF16),
                dma((2,)),
                dma((2, 2)), dma((2, 2)),
                dma((2,)), dma((2,)),
                dma((2, len(FAR_CUTS))), dma((2, len(FAR_CUTS))),
                dma((2,)), dma((2,)),
                dma((2, 2)), dma((2, 2)),
            ],
            compiler_params=pltpu.CompilerParams(
                collective_id=0, has_side_effects=True, vmem_limit_bytes=56 * 2**20
            ),
            cost_estimate=pl.CostEstimate(
                flops=13_000_000_000, bytes_accessed=4_000_000, transcendentals=0
            ),
            name="disco",
        )(field, filters, filter_scales, lon_offsets, lon_widths, halo_rows, mixing)

    return jax.shard_map(
        on_device,
        mesh=mesh,
        in_specs=(
            P("lat", "lon", None),
            P("lat", None, None, None),
            P("lat", None),
            P("lat"),
            P("lat"),
            P("lat"),
            P(),
        ),
        out_specs=P("lat", "lon", None),
        check_vma=False,
    )
```

```python
import functools

import jax
import jax.numpy as jnp
from jax import lax
from jax.experimental import pallas as pl
from jax.experimental.pallas import tpu as pltpu
from jax.sharding import PartitionSpec as P

MESH = pl.DeviceIdType.MESH
BASIS = 9
TAPS = 5
HROWS = 2
REACH = 64
SPAN = 2 * REACH
BLOCK = 32
F32 = jnp.float32
BF16 = jnp.bfloat16

OWN_TAPS = ((2, 3, 4), (1, 2, 3, 4), (0, 1, 2, 3), (0, 1, 2))
AWAY_TAPS = ((0, 1), (0,), (4,), (3, 4))
FAR_CUTS = ((64, 160), (224, 160), (384, 32))
STAGES = ((2, 5), (5, 10), (10, 15))


def kernel(
    n_lat, n_lon,
    x_ref, f_ref, s_ref, off_ref, wid_ref, halo_ref, w_hbm, out,
    ext, lines, moved, a_own, a_away, acc, conv, tail, edge, w_ref,
    own_sem, edge_s, edge_r, near_s, near_r, far_s, far_r, lon_s, lon_r, rel_s, rel_r,
):
    rows, cols, chans = x_ref.shape
    la, lo = lax.axis_index("lat"), lax.axis_index("lon")
    west, east = lax.rem(lo + n_lon - 1, n_lon), lax.rem(lo + 1, n_lon)
    has_n, has_s = la > 0, la < n_lat - 1
    far_cuts = FAR_CUTS

    barrier = pltpu.get_barrier_semaphore()
    for lon in (west, east):
        pl.semaphore_signal(barrier, inc=1, device_id=(la, lon), device_id_type=MESH)

    @pl.when(has_n)
    def _():
        pl.semaphore_signal(barrier, inc=1, device_id=(la - 1, lo), device_id_type=MESH)

    @pl.when(has_s)
    def _():
        pl.semaphore_signal(barrier, inc=1, device_id=(la + 1, lo), device_id_type=MESH)

    own = pltpu.make_async_copy(
        x_ref, ext.at[pl.ds(HROWS, rows), pl.ds(REACH, cols)], own_sem.at[0]
    )
    own.start()
    weights = pltpu.make_async_copy(w_hbm, w_ref, own_sem.at[1])
    weights.start()

    tall = BASIS * BLOCK
    lane = lax.broadcasted_iota(jnp.int32, (BLOCK, SPAN), 1)
    step = lax.broadcasted_iota(jnp.int32, (BLOCK, SPAN), 0)
    entry = lax.broadcasted_iota(jnp.int32, (SPAN, SPAN), 0)
    place = lax.broadcasted_iota(jnp.int32, (SPAN, SPAN), 1)
    n_lines = lines.shape[0]
    line_at = lax.broadcasted_iota(jnp.int32, (n_lines, SPAN), 0)
    line_tap = (line_at - line_at // (TAPS * rows) * (TAPS * rows)) // rows

    lines[n_lines - 8:] = jnp.zeros((8, SPAN), F32)
    for k in range(BASIS):
        for t in range(TAPS):
            at = (k * TAPS + t) * rows
            lines[at:at + rows] = f_ref[k, t].astype(F32)
    for i in range(rows):
        hit = (place == entry + off_ref[i] + REACH) & (entry < wid_ref[i])
        mover = jnp.where(hit, 1.0, 0.0).astype(BF16)
        shifted = jnp.dot(lines[...].astype(BF16), mover, preferred_element_type=F32)
        moved[i] = jnp.where(jnp.abs(line_tap - HROWS) <= halo_ref[i], shifted, 0.0)

    def unit(ref, i, j, k, taps):
        at = k * BLOCK
        rest = jnp.zeros((BLOCK, SPAN), F32)
        for u, t in enumerate(taps):
            row = (k * TAPS + t) * rows + i
            line = jnp.broadcast_to(moved[i, row:row + 1], (BLOCK, SPAN))
            skew = pltpu.roll(line, 0, 1, stride=1, stride_axis=0)
            head = jnp.where(lane >= step, skew, 0.0)
            ref[j, at:at + BLOCK, u * SPAN:(u + 1) * SPAN] = head.astype(BF16)
            spot = lane - u * BLOCK
            turned = pltpu.roll(skew, u * BLOCK, 1) if u else skew
            rest = jnp.where((spot >= 0) & (spot < step), turned, rest)
        n = len(taps)
        ref[j, at:at + BLOCK, n * SPAN:(n + 1) * SPAN] = rest.astype(BF16)

    for i in range(rows):
        for k in range(BASIS):
            unit(a_own, i, i, k, OWN_TAPS[i])
            unit(a_away, i, i, k, AWAY_TAPS[i])

    peers = 2 + jnp.where(has_n, 1, 0) + jnp.where(has_s, 1, 0)
    pl.semaphore_wait(barrier, peers)

    def lat_copy(d, near, far, at, size, send, recv):
        src, dst, to = ((rows - 2, 0, la + 1), (0, rows + HROWS, la - 1))[d]
        skip, count = (0, 2) if near and far else ((1 - d, 1) if near else (d, 1))
        return pltpu.make_async_remote_copy(
            x_ref.at[pl.ds(src + skip, count), pl.ds(at, size)],
            ext.at[pl.ds(dst + skip, count), pl.ds(REACH + at, size)],
            send, recv, device_id=(to, lo), device_id_type=MESH,
        )

    def edge_copy(d, e):
        at = (0, cols - REACH)[e]
        return lat_copy(d, True, True, at, REACH, edge_s.at[d, e], edge_r.at[d, e])

    def near_copy(d):
        return lat_copy(d, True, False, REACH, cols - SPAN, near_s.at[d], near_r.at[d])

    def far_copy(d, p):
        at, size = far_cuts[p]
        return lat_copy(d, False, True, at, size, far_s.at[d, p], far_r.at[d, p])

    def lon_copy(d):
        at, to, land = ((cols - REACH, east, 0), (0, west, cols + REACH))[d]
        return pltpu.make_async_remote_copy(
            x_ref.at[:, pl.ds(at, REACH)], ext.at[pl.ds(HROWS, rows), pl.ds(land, REACH)],
            lon_s.at[d], lon_r.at[d], device_id=(la, to), device_id_type=MESH,
        )

    def relay(d, e):
        row = (0, rows + HROWS)[d]
        at, to, land = ((cols, east, 0), (REACH, west, cols + REACH))[e]
        return pltpu.make_async_remote_copy(
            ext.at[pl.ds(row, HROWS), pl.ds(at, REACH)],
            ext.at[pl.ds(row, HROWS), pl.ds(land, REACH)],
            rel_s.at[d, e], rel_r.at[d, e], device_id=(la, to), device_id_type=MESH,
        )

    sends = (has_s, has_n)
    comes = (has_n, has_s)
    pieces = range(len(far_cuts))

    def guarded(conds, action):
        for d in range(2):
            @pl.when(conds[d])
            def _():
                action(d)

    for d in range(2):
        lon_copy(d).start()
    for e in range(2):
        guarded(sends, lambda d: edge_copy(d, e).start())
    guarded(sends, lambda d: near_copy(d).start())
    for p in pieces:
        guarded(sends, lambda d: far_copy(d, p).start())

    @pl.when(jnp.logical_not(has_n))
    def _():
        ext[0:HROWS] = jnp.zeros((HROWS, cols + SPAN, chans), BF16)

    @pl.when(jnp.logical_not(has_s))
    def _():
        ext[rows + HROWS:] = jnp.zeros((HROWS, cols + SPAN, chans), BF16)

    def window(rows_in, b):
        at = b * BLOCK
        heads = [ext[r, at:at + SPAN] for r in rows_in]
        rests = [ext[r, at + SPAN:at + SPAN + BLOCK] for r in rows_in]
        return jnp.concatenate(heads + rests, 0)

    def part(ref, i, taps, b):
        depth = len(taps) * (SPAN + BLOCK)
        return jnp.dot(
            ref[i, :, 0:depth], window([i + t for t in taps], b), preferred_element_type=F32
        )

    def own_part(i, b):
        acc[i, b] = part(a_own, i, OWN_TAPS[i], b)

    def finish(i, b, ref, at):
        total = acc[i, b] + part(a_away, i, AWAY_TAPS[i], b)
        for k in range(BASIS):
            scaled = total[k * BLOCK:(k + 1) * BLOCK] * s_ref[i, k]
            ref[at:at + BLOCK, k * chans:(k + 1) * chans] = scaled.astype(BF16)

    blocks = cols // BLOCK
    inner = range(REACH // BLOCK, blocks - REACH // BLOCK)
    outer = [b for b in range(blocks) if b not in inner]
    own.wait()
    for b in inner:
        own_part(0, b)
        own_part(3, b)

    def pass_edges(d):
        for e in range(2):
            edge_copy(d, e).wait_recv()
        for e in range(2):
            relay(d, e).start()

    guarded(comes, pass_edges)

    for b in inner:
        own_part(1, b)
        own_part(2, b)

    weights.wait()
    guarded(comes, lambda d: near_copy(d).wait_recv())
    n_in = len(inner) * BLOCK
    for n, b in enumerate(inner):
        finish(1, b, conv, n * BLOCK)
        finish(2, b, conv, n_in + n * BLOCK)

    def mix(ref, at, size, lands):
        mixed = jnp.dot(ref[at:at + size], w_ref[...], preferred_element_type=F32).astype(BF16)
        at = 0
        for i, b, count in lands:
            out[i, b * BLOCK:(b + count) * BLOCK] = mixed[at:at + count * BLOCK]
            at += count * BLOCK

    def take_corners(d):
        for e in range(2):
            relay(d, e).wait_recv()

    for g, (lo_b, hi_b) in enumerate(STAGES[:-1]):
        guarded(comes, lambda d: far_copy(d, g).wait_recv())
        count = hi_b - lo_b
        for b in range(lo_b, hi_b):
            finish(0, b, tail, (b - lo_b) * BLOCK)
            finish(3, b, tail, (count + b - lo_b) * BLOCK)
        if g == 0:
            mix(conv, 0, n_in, [(1, inner[0], len(inner))])
            mix(conv, n_in, n_in, [(2, inner[0], len(inner))])
        for n, i in enumerate((0, 3)):
            mix(tail, n * count * BLOCK, count * BLOCK, [(i, lo_b, count)])

    for d in range(2):
        lon_copy(d).wait_recv()
    for b in outer:
        for i in range(rows):
            own_part(i, b)

    guarded(comes, take_corners)
    side = inner[0]
    lo_b, hi_b = STAGES[-1]
    ends = list(range(lo_b, hi_b)) + list(range(side))
    base = len(outer)
    half = (base + len(ends)) * BLOCK
    for n, b in enumerate(outer):
        finish(1, b, edge, n * BLOCK)
        finish(2, b, edge, half + n * BLOCK)
    guarded(comes, lambda d: far_copy(d, len(STAGES) - 1).wait_recv())
    for n, b in enumerate(ends):
        finish(0, b, edge, (base + n) * BLOCK)
        finish(3, b, edge, half + (base + n) * BLOCK)
    for at, i, j in ((0, 1, 0), (half, 2, 3)):
        mix(edge, at, half,
            [(i, 0, side), (i, blocks - side, side), (j, lo_b, hi_b - lo_b), (j, 0, side)])

    def drain(d):
        for e in range(2):
            edge_copy(d, e).wait_send()
        near_copy(d).wait_send()
        for p in pieces:
            far_copy(d, p).wait_send()

    guarded(sends, drain)
    for d in range(2):
        lon_copy(d).wait_send()

    def drain_relays(d):
        for e in range(2):
            relay(d, e).wait_send()

    guarded(comes, drain_relays)


def solution(mesh):
    n_lat, n_lon = mesh.shape["lat"], mesh.shape["lon"]

    def on_device(field, filter_blocks, filter_scales, lon_offsets, lon_widths, halo_rows, mixing):
        rows, cols, chans = field.shape
        outs = mixing.shape[1]
        wide = cols + SPAN
        blocks = cols // BLOCK
        tall = BASIS * BLOCK
        n_lines = -(-BASIS * TAPS * rows // 8) * 8
        smem = pl.BlockSpec(memory_space=pltpu.SMEM)
        hbm = pl.BlockSpec(memory_space=pl.ANY)
        dma = pltpu.SemaphoreType.DMA
        filters = jnp.transpose(filter_blocks, (1, 2, 0, 3))
        return pl.pallas_call(
            functools.partial(kernel, n_lat, n_lon),
            out_shape=pltpu.VMEM((rows, cols, outs), BF16),
            in_specs=[hbm, pl.BlockSpec(memory_space=pltpu.VMEM), smem, smem, smem, smem, hbm],
            out_specs=pl.BlockSpec(memory_space=pltpu.VMEM),
            scratch_shapes=[
                pltpu.VMEM((rows + 2 * HROWS, wide, chans), BF16),
                pltpu.VMEM((n_lines, SPAN), F32),
                pltpu.VMEM((rows, n_lines, SPAN), F32),
                pltpu.VMEM((rows, tall, 5 * SPAN), BF16),
                pltpu.VMEM((rows, tall, 3 * SPAN), BF16),
                pltpu.VMEM((rows, blocks, tall, chans), F32),
                pltpu.VMEM((2 * (cols - SPAN), BASIS * chans), BF16),
                pltpu.VMEM((2 * 5 * BLOCK, BASIS * chans), BF16),
                pltpu.VMEM((22 * BLOCK, BASIS * chans), BF16),
                pltpu.VMEM((BASIS * chans, outs), BF16),
                dma((2,)),
                dma((2, 2)), dma((2, 2)),
                dma((2,)), dma((2,)),
                dma((2, len(FAR_CUTS))), dma((2, len(FAR_CUTS))),
                dma((2,)), dma((2,)),
                dma((2, 2)), dma((2, 2)),
            ],
            compiler_params=pltpu.CompilerParams(
                collective_id=0, has_side_effects=True, vmem_limit_bytes=56 * 2**20
            ),
            cost_estimate=pl.CostEstimate(
                flops=13_000_000_000, bytes_accessed=4_000_000, transcendentals=0
            ),
            name="disco",
        )(field, filters, filter_scales, lon_offsets, lon_widths, halo_rows, mixing)

    return jax.shard_map(
        on_device,
        mesh=mesh,
        in_specs=(
            P("lat", "lon", None),
            P("lat", None, None, None),
            P("lat", None),
            P("lat"),
            P("lat"),
            P("lat"),
            P(),
        ),
        out_specs=P("lat", "lon", None),
        check_vma=False,
    )
```
